32 devices in a mesh: parts: 1, ctx: 32 (over z, y, x, core).
Axes of the slice: x: 2, y: 2, z: 4, core: 2. Of those that a mesh axis runs over, the one named last changes fastest.
Arguments:
- q_lin: bfloat16 [2048, 4096], P(('parts', 'ctx')), may hold values from -6 to 6
- k_lin: bfloat16 [2048, 4096], P(('parts', 'ctx')), may hold values from -6 to 6
- v_lin: bfloat16 [2048, 4096], P(('parts', 'ctx')), may hold values from -6 to 6
- log_decay: float32 [2048, 32], P(('parts', 'ctx')), may hold values from -2 to 0
- pattern: int32 [64, 2], P(('parts', 'ctx')), may hold values 0 or 1
- q_soft: bfloat16 [2048, 4096], P(('parts', 'ctx')), may hold values from -64 to 64
- k_soft: bfloat16 [2048, 512], P(('parts', 'ctx')), may hold values from -4 to 4
- v_soft: bfloat16 [2048, 512], P(('parts', 'ctx')), may hold values from -6 to 6
Outputs:
- lightning_out: bfloat16 [2048, 4096], P(('parts', 'ctx'))
- softmax_out: bfloat16 [2048, 4096], P(('parts', 'ctx'))
The draws below stay inside these ranges and needn't reach their ends.
All inputs are finite; a program needn't handle non-finite values. No bound on the sum of `pattern` on one device may be relied on, other than what follows from the above.
Results may differ from the reference program's by a relative error of at most 0.012.
Values may be sent and summed in bfloat16 or wider, within the bound.
A program may use at most 320 MiB of HBM per device.

```python
import math
import jax
import jax.numpy as jnp
from jax import lax

DH = 128
LIGHTNING_HEADS = 32
HQ = 32
KVH = 4
BLK = 32
TOK_DEV = 64
NB = 2
SEQUENCE_LENGTH = 2048


def shared_keys(key):
    normal_part = jnp.clip(jax.random.normal(jax.random.fold_in(key, 101), (SEQUENCE_LENGTH, KVH * DH), jnp.float32), -4.0, 4.0)
    return normal_part


def span_loudness(key):
    spans = SEQUENCE_LENGTH // TOK_DEV
    gain = jnp.exp(jax.random.uniform(key, (spans, LIGHTNING_HEADS), jnp.float32, -2.5, 1.0))
    gain = jnp.repeat(gain, TOK_DEV, axis=0)
    return jnp.repeat(gain, DH, axis=1)


def loud_field(key):
    gain = span_loudness(jax.random.fold_in(key, 1))
    raw = jax.random.normal(jax.random.fold_in(key, 2), (SEQUENCE_LENGTH, LIGHTNING_HEADS * DH), jnp.float32)
    return jnp.clip(gain * raw, -6.0, 6.0)


def draw_k_lin(key, part):
    key = jax.random.fold_in(key, 21)
    field = loud_field(key)
    return field.astype(jnp.bfloat16)


def draw_v_lin(key, part):
    key = jax.random.fold_in(key, 22)
    field = loud_field(key)
    return field.astype(jnp.bfloat16)


def draw_k_soft(key, part):
    base = shared_keys(key)
    return base.astype(jnp.bfloat16)


def draw_q_soft(key, part):
    key = jax.random.fold_in(key, 9)
    final_output = jnp.clip(jax.random.normal(key, (SEQUENCE_LENGTH, HQ * DH), jnp.float32), -6.0, 6.0)
    return final_output.astype(jnp.bfloat16)


def draw_log_decay(key, part):
    key = jax.random.fold_in(key, 7)
    fast_share = 0.3
    middle_share = 0.35
    spans = SEQUENCE_LENGTH // TOK_DEV
    choose = jax.random.uniform(jax.random.fold_in(key, 1), (LIGHTNING_HEADS,), jnp.float32)
    forced = jax.random.randint(jax.random.fold_in(key, 9), (), 0, LIGHTNING_HEADS)
    fast_rate = jnp.exp(jax.random.uniform(jax.random.fold_in(key, 2), (LIGHTNING_HEADS,), jnp.float32, jnp.log(1.5), jnp.log(3.0))) / TOK_DEV
    middle_rate = jnp.exp(jax.random.uniform(jax.random.fold_in(key, 10), (LIGHTNING_HEADS,), jnp.float32, jnp.log(0.15), jnp.log(0.6))) / TOK_DEV
    slow_rate = 0.3 / SEQUENCE_LENGTH * jax.random.uniform(jax.random.fold_in(key, 3), (LIGHTNING_HEADS,), jnp.float32, 0.5, 1.5)
    decay_rate = jnp.where(choose < fast_share, fast_rate, jnp.where(choose < fast_share + middle_share, middle_rate, slow_rate))
    decay_rate = jnp.where(jnp.arange(LIGHTNING_HEADS) == forced, slow_rate, decay_rate)
    segment_decay_factor = jnp.exp(jax.random.uniform(jax.random.fold_in(key, 4), (spans, LIGHTNING_HEADS), jnp.float32, jnp.log(0.5), jnp.log(1.5)))
    segment_decay_factor = jnp.repeat(segment_decay_factor, TOK_DEV, axis=0)
    per_token_decay = jax.random.uniform(jax.random.fold_in(key, 5), (SEQUENCE_LENGTH, LIGHTNING_HEADS), jnp.float32, 0.5, 1.5)
    selected_spike = jax.random.uniform(jax.random.fold_in(key, 6), (SEQUENCE_LENGTH, LIGHTNING_HEADS), jnp.float32) < 3.0 / SEQUENCE_LENGTH
    retained_spike = jax.random.uniform(jax.random.fold_in(key, 8), (SEQUENCE_LENGTH, LIGHTNING_HEADS), jnp.float32, 0.5, 0.8)
    final_output = -decay_rate[None, :] * segment_decay_factor * per_token_decay + jnp.where(selected_spike, jnp.log(retained_spike), 0.0)
    return final_output.astype(jnp.float32)


def touch_ends(array, key, least, largest):
    index_at = [jax.random.randint(jax.random.fold_in(key, axis), (), 0, length) for axis, length in enumerate(array.shape)]
    longest = array.shape.index(max(array.shape))
    next_to = index_at[:longest] + [(index_at[longest] + 1) % array.shape[longest]] + index_at[longest + 1:]
    return array.at[tuple(index_at)].set(least).at[tuple(next_to)].set(largest)


def level_of(key, extent, split, smallest, largest):
    level = 1.0
    for dim, shards_of in split:
        heights = jax.random.uniform(jax.random.fold_in(jax.random.fold_in(key, 6), dim), (shards_of,), jnp.float32, smallest / len(split), largest / len(split))
        level = level * jnp.repeat(jnp.exp(heights), extent[dim] // shards_of).reshape((-1,) + (1,) * (len(extent) - 1 - dim))
    return level


def centred(key, extent, scale, limit, shards=(), kind=jnp.bfloat16):
    drawn = scale * jax.random.normal(key, extent, jnp.float32)
    if shards:
        drawn = drawn * level_of(key, extent, shards, -0.22, 0.18)
    return jnp.clip(drawn, -limit, limit).astype(kind)


def setup_inputs(seed: int = 0, part: int = 0) -> dict:
    seeds = jax.random.split(jax.random.key(seed), 9)
    part_splits = jax.random.split(jax.random.fold_in(seeds[8], part), 9)
    q_lin = centred(part_splits[0], (SEQUENCE_LENGTH, LIGHTNING_HEADS * DH), 1.0, 6.0, ((0, 32),))
    k_lin = draw_k_lin(jax.random.fold_in(jax.random.fold_in(seeds[8], part), 71), part)
    v_lin = draw_v_lin(jax.random.fold_in(jax.random.fold_in(seeds[8], part), 71), part)
    log_decay = draw_log_decay(jax.random.fold_in(jax.random.fold_in(seeds[8], part), 71), part)
    pattern = touch_ends((jax.random.randint(part_splits[4], (SEQUENCE_LENGTH // BLK, NB), 0, 2) < 1).astype(jnp.int32), jax.random.fold_in(part_splits[4], 1), 0, 1)
    q_soft = draw_q_soft(jax.random.fold_in(jax.random.fold_in(seeds[8], part), 71), part)
    k_soft = draw_k_soft(jax.random.fold_in(jax.random.fold_in(seeds[8], part), 71), part)
    v_soft = centred(part_splits[7], (SEQUENCE_LENGTH, KVH * DH), 1.0, 6.0, ((0, 32),))
    return dict(q_lin=q_lin, k_lin=k_lin, v_lin=v_lin, log_decay=log_decay, pattern=pattern, q_soft=q_soft, k_soft=k_soft, v_soft=v_soft)


def lightning_span(q, k, v, ell, state, pat):
    tok = q.shape[0]
    inter = jnp.einsum('thd,hde->the', q.astype(jnp.float32), state.astype(jnp.float32)) * jnp.exp(ell)[:, :, None]
    scores = jnp.einsum('thd,shd->hts', q.astype(jnp.float32), k.astype(jnp.float32))
    blocks = pat.shape[0]
    index = jnp.arange(blocks)
    allowed = (pat == 1) & (index[None, :] < index[:, None]) | (index[:, None] == index[None, :])
    width = tok // blocks
    block_mask = jnp.broadcast_to(allowed[:, None, :, None], (blocks, width, blocks, width)).reshape(tok, tok)
    position = jnp.arange(tok)
    live = block_mask & (position[None, :] <= position[:, None])
    ell_heads = ell.T
    diff = ell_heads[:, :, None] - ell_heads[:, None, :]
    decay = jnp.where(live[None], jnp.exp(jnp.where(live[None], diff, 0.0)), 0.0)
    weights = (scores * decay).astype(jnp.bfloat16)
    intra = jnp.einsum('hts,she->the', weights.astype(jnp.float32), v.astype(jnp.float32))
    mixed = inter + intra
    normed = mixed / jnp.sqrt(lax.optimization_barrier(jnp.mean(mixed * mixed, axis=-1, keepdims=True)) + 1e-06)
    return normed.astype(jnp.bfloat16).reshape(tok, -1)

def reference(q_lin, k_lin, v_lin, log_decay, pattern, q_soft, k_soft, v_soft):
    spans = SEQUENCE_LENGTH // TOK_DEV
    q = q_lin.reshape(spans, TOK_DEV, LIGHTNING_HEADS, DH)
    k = k_lin.reshape(spans, TOK_DEV, LIGHTNING_HEADS, DH)
    v = v_lin.reshape(spans, TOK_DEV, LIGHTNING_HEADS, DH)
    ell = jnp.cumsum(log_decay.reshape(spans, TOK_DEV, LIGHTNING_HEADS), axis=1)
    ell_end = ell[:, -1, :]
    decayed = (k.astype(jnp.float32) * jnp.exp(ell_end[:, None, :] - ell)[..., None]).astype(jnp.bfloat16)
    summary = jnp.einsum('cthd,cthe->chde', decayed.astype(jnp.float32), v.astype(jnp.float32))
    decay_end = jnp.exp(ell_end)

    def advance(state, inputs):
        factor, term = inputs
        return (factor[:, None, None] * state + term, state)
    start_state = jnp.zeros((LIGHTNING_HEADS, DH, DH), jnp.float32)
    _, state_in = lax.scan(advance, start_state, (decay_end, summary))
    state_round = state_in.astype(jnp.bfloat16)
    pat = pattern.reshape(spans, NB, NB)

    def one_span(inputs):
        return lightning_span(*inputs)
    lightning_out = lax.map(one_span, (q, k, v, ell, state_round, pat)).reshape(SEQUENCE_LENGTH, LIGHTNING_HEADS * DH)
    group = HQ // KVH
    scale = 1.0 / math.sqrt(DH)
    queries = q_soft.reshape(spans, TOK_DEV, KVH, group, DH)
    keys = k_soft.reshape(SEQUENCE_LENGTH, KVH, DH).astype(jnp.float32)
    values = v_soft.reshape(SEQUENCE_LENGTH, KVH, DH).astype(jnp.float32)
    key_pos = jnp.arange(SEQUENCE_LENGTH)

    def soft_span(inputs):
        query, span = inputs
        scores = jnp.einsum('tkgd,skd->kgts', query.astype(jnp.float32), keys) * scale
        query_pos = span * TOK_DEV + jnp.arange(TOK_DEV)
        live = key_pos[None, :] <= query_pos[:, None]
        top = lax.optimization_barrier(jnp.max(jnp.where(live, scores, -1e+30), axis=-1))
        probs = jnp.where(live, jnp.exp(scores - top[..., None]), 0.0)
        total = lax.optimization_barrier(jnp.sum(probs, axis=-1))
        out = jnp.einsum('kgts,skd->kgtd', probs.astype(jnp.bfloat16).astype(jnp.float32), values) / total[..., None]
        return jnp.transpose(out, (2, 0, 1, 3)).reshape(TOK_DEV, HQ * DH).astype(jnp.bfloat16)
    span_ids = jnp.arange(spans).astype(jnp.int32)
    softmax_out = lax.map(soft_span, (queries, span_ids)).reshape(SEQUENCE_LENGTH, HQ * DH)
    return (lightning_out, softmax_out)
```

```python
import functools
import math

import jax
import jax.numpy as jnp
from jax import lax
from jax.experimental import pallas as pl
from jax.experimental.pallas import tpu as pltpu
from jax.sharding import PartitionSpec as P

DH = 128
HQ = 32
KVH = 4
PLANE = 8
CHIPS = 4
NEG = -1e30
F32 = jnp.float32
BF16 = jnp.bfloat16


def dot(a, b, dims, precision=None):
    return lax.dot_general(
        a, b, (dims, ((), ())), precision=precision, preferred_element_type=F32
    )


def kernel(
    planes,
    q_lin,
    k_lin,
    v_lin,
    log_decay,
    pattern,
    q_soft,
    k_soft,
    v_soft,
    lin_out,
    soft_out,
    kv,
    ends,
    sums,
    gathered,
    totals,
    total_ends,
    prefix,
    outgoing,
    state,
    mixed,
    ell_ref,
    ell_rows,
    queries,
    top_ref,
    den_ref,
    acc_ref,
    kv_recv,
    col_send,
    in_send,
    sib_send,
    end_send,
    end_recv,
    sum_send,
    sum_recv,
    tot_send,
    tot_recv,
    tend_send,
    tend_recv,
    st_send,
    st_recv,
):
    tok = q_lin.shape[0]
    heads = log_decay.shape[1]
    per = heads // PLANE
    blocks = pattern.shape[1]
    width = tok // blocks
    kvw = k_soft.shape[1]
    group = HQ // KVH
    rows = group * tok
    me = lax.axis_index("ctx")
    z, j = me // PLANE, lax.rem(me, PLANE)
    chip, core = j // 2, lax.rem(j, 2)
    base = z * PLANE
    sibling = base + chip * 2 + (1 - core)

    def remote(src, dst, send, recv, device):
        return pltpu.make_async_remote_copy(
            src_ref=src,
            dst_ref=dst,
            send_sem=send,
            recv_sem=recv,
            device_id={"ctx": device},
            device_id_type=pl.DeviceIdType.MESH,
        )

    def span(s):
        return kv.at[s]

    def kv_copy(s, send, device):
        return remote(span(s), span(s), send, kv_recv.at[s], device)

    def other_chip(o):
        return lax.rem(chip + o, CHIPS)

    kv[me, :, :kvw] = k_soft[...]
    kv[me, :, kvw:] = v_soft[...]
    for p in range(PLANE):
        @pl.when(p > j)
        def _():
            kv[base + p] = jnp.zeros((tok, 2 * kvw), BF16)

    barrier = pltpu.get_barrier_semaphore()
    for o in range(1, PLANE):
        pl.semaphore_signal(
            barrier, inc=1, device_id={"ctx": base + lax.rem(j + o, PLANE)},
            device_id_type=pl.DeviceIdType.MESH,
        )
    for o in range(1, planes):
        pl.semaphore_signal(
            barrier, inc=1, device_id={"ctx": lax.rem(z + o, planes) * PLANE + j},
            device_id_type=pl.DeviceIdType.MESH,
        )
    pl.semaphore_wait(barrier, PLANE - 1 + planes - 1)

    def column(up, wait):
        copy = kv_copy(me, col_send.at[up], up * PLANE + j)
        copy.wait_send() if wait else copy.start()

    def column_all(wait):
        def body(up, c):
            column(up, wait)
            return c

        lax.fori_loop(z + 1, planes, body, 0)

    def own_row(wait):
        for o in range(1, CHIPS):
            k2 = other_chip(o)

            @pl.when(k2 > chip)
            def _():
                copy = kv_copy(me, in_send.at[z, o - 1], base + k2 * 2 + core)
                copy.wait_send() if wait else copy.start()

        @pl.when(core == 0)
        def _():
            copy = kv_copy(me, sib_send.at[z, 0], sibling)
            copy.wait_send() if wait else copy.start()

    def lower_row(r, wait):
        s = r * PLANE + j
        if not wait:
            kv_copy(s, col_send.at[r], me).wait_recv()
        for o in range(1, CHIPS):
            copy = kv_copy(s, in_send.at[r, o - 1], base + other_chip(o) * 2 + core)
            copy.wait_send() if wait else copy.start()
        copy = kv_copy(s, sib_send.at[r, 0], sibling)
        copy.wait_send() if wait else copy.start()

    def forward_row(r, wait):
        for o in range(1, CHIPS):
            s = r * PLANE + other_chip(o) * 2 + core
            if not wait:
                kv_copy(s, sib_send.at[r, o], sibling).wait_recv()
            copy = kv_copy(s, sib_send.at[r, o], sibling)
            copy.wait_send() if wait else copy.start()

    def forward_own(wait):
        for o in range(1, CHIPS):
            k2 = other_chip(o)

            @pl.when(k2 < chip)
            def _():
                s = base + k2 * 2 + core
                copy = kv_copy(s, sib_send.at[z, o], sibling)
                if not wait:
                    copy.wait_recv()
                copy.wait_send() if wait else copy.start()

    column_all(False)
    own_row(False)

    t_pos = lax.broadcasted_iota(jnp.int32, (tok, tok), 0)
    s_pos = lax.broadcasted_iota(jnp.int32, (tok, tok), 1)
    causal = s_pos <= t_pos
    tri = causal.astype(F32)
    high = lax.Precision.HIGHEST
    decay = log_decay[...]
    ell_ref[...] = dot(tri, decay, ((1,), (0,)), high)
    ell_rows[...] = dot(decay, tri, ((0,), (1,)), high)
    ends[j] = dot(decay, jnp.ones((tok, DH), F32), ((0,), (0,)), high)

    def end_copy(o):
        return remote(
            ends.at[j], ends.at[j], end_send.at[o], end_recv.at[j],
            base + lax.rem(j + o, PLANE),
        )

    for o in range(1, PLANE):
        end_copy(o).start()

    lane = lax.broadcasted_iota(jnp.int32, (tok, heads), 1)

    def column_of(h):
        return jnp.sum(jnp.where(lane == h, ell_ref[...], 0.0), axis=1, keepdims=True)

    def columns(h):
        return pl.ds(pl.multiple_of(h * DH, DH), DH)

    def sum_copy(o):
        g = lax.rem(j + o, PLANE)
        return remote(sums.at[g], gathered.at[j], sum_send.at[g], sum_recv.at[j], base + g)

    def summarize(i, c):
        g = lax.rem(j + i, PLANE)
        for u in range(per):
            h = g * per + u
            col = column_of(h)
            scaled = k_lin[:, columns(h)].astype(F32) * jnp.exp(col[tok - 1 : tok, :] - col)
            total = dot(scaled.astype(BF16), v_lin[:, columns(h)], ((0,), (0,)))
            sums[g, u * DH : (u + 1) * DH, :] = total.astype(BF16)

        @pl.when(i < PLANE)
        def _():
            sum_copy(i).start()

        return c

    lax.fori_loop(1, PLANE + 1, summarize, 0)
    gathered[j] = sums[j]

    def send_lower(r, c):
        lower_row(r, False)
        return c

    lax.fori_loop(0, z, send_lower, 0)

    t_blk, s_blk = t_pos // width, s_pos // width
    live = t_blk == s_blk
    for b in range(blocks):
        for a in range(b):
            live = live | (
                (t_blk == b) & (s_blk == a) & (pattern[b : b + 1, a : a + 1] == 1)
            )
    live = live & causal

    def within(g, c):
        for u in range(per):
            h = g * per + u
            cols = columns(h)
            scores = dot(q_lin[:, cols], k_lin[:, cols], ((1,), (1,)))
            diff = column_of(h) - ell_rows[pl.ds(h, 1), :]
            weight = jnp.where(live, scores * jnp.exp(jnp.where(live, diff, 0.0)), 0.0)
            mixed[:, cols] = dot(weight.astype(BF16), v_lin[:, cols], ((1,), (0,)))
        return c

    lax.fori_loop(0, PLANE, within, 0)

    for kh in range(KVH):
        for g in range(group):
            h = kh * group + g
            queries[kh, g * tok : (g + 1) * tok, :] = q_soft[:, h * DH : (h + 1) * DH]

    for o in range(1, PLANE):
        c = lax.rem(j + o, PLANE)
        remote(ends.at[c], ends.at[c], end_send.at[o], end_recv.at[c], me).wait_recv()
        remote(sums.at[c], gathered.at[c], sum_send.at[c], sum_recv.at[c], me).wait_recv()

    def scan(u, carry):
        at = pl.ds(pl.multiple_of(u * DH, DH), DH)
        run = jnp.zeros((DH, DH), F32)
        for c in range(PLANE):
            prefix[c, at, :] = run
            run = run * jnp.exp(ends[c, pl.ds(j * per + u, 1), :]) + gathered[c, at, :].astype(F32)
        totals[z, at, :] = run.astype(BF16)
        return carry

    lax.fori_loop(0, per, scan, 0)
    plane_end = ends[0]
    for c in range(1, PLANE):
        plane_end = plane_end + ends[c]
    total_ends[z] = plane_end

    def total_copies(up):
        device = up * PLANE + j
        return (
            remote(totals.at[z], totals.at[z], tot_send.at[up], tot_recv.at[z], device),
            remote(total_ends.at[z], total_ends.at[z], tend_send.at[up], tend_recv.at[z], device),
        )

    def send_totals(up, c):
        for copy in total_copies(up):
            copy.start()
        return c

    lax.fori_loop(z + 1, planes, send_totals, 0)

    factor = math.log2(math.e) / math.sqrt(DH)

    def fold(r, kh, first):
        at = pl.ds(pl.multiple_of(r * PLANE, PLANE), PLANE)
        keys = kv[at, :, kh * DH : (kh + 1) * DH].reshape(PLANE * tok, DH)
        values = kv[at, :, kvw + kh * DH : kvw + (kh + 1) * DH].reshape(PLANE * tok, DH)
        scores = dot(keys, queries[kh], ((1,), (1,)))
        if first:
            shape = (PLANE * tok, tok)
            key = lax.broadcasted_iota(jnp.int32, shape, 0)
            query = j * tok + lax.broadcasted_iota(jnp.int32, shape, 1)
            bias = jnp.where(key <= query, 0.0, NEG)
            scores = scores + jnp.concatenate([bias] * group, axis=1)
            top = jnp.max(scores, axis=0, keepdims=True)
        else:
            old = top_ref[kh]
            top = jnp.maximum(old, jnp.max(scores, axis=0, keepdims=True))
        probs = jnp.exp2(scores * factor - top * factor)
        den = jnp.sum(probs, axis=0, keepdims=True)
        acc = dot(values, probs.astype(BF16), ((0,), (0,)))
        if not first:
            shrink = jnp.exp2((old - top) * factor)
            den = den + den_ref[kh] * shrink
            acc = acc + acc_ref[kh] * shrink
        top_ref[kh] = top
        den_ref[kh] = den
        acc_ref[kh] = acc

    forward_own(False)
    for k2 in range(CHIPS):
        @pl.when((k2 < chip) | ((k2 == chip) & (core == 1)))
        def _():
            s = base + k2 * 2 + (1 - core)
            kv_copy(s, sib_send.at[z, 0], me).wait_recv()

    for kh in range(KVH):
        fold(z, kh, True)

    def take_totals(low, c):
        remote(totals.at[low], totals.at[low], tot_send.at[low], tot_recv.at[low], me).wait_recv()
        remote(
            total_ends.at[low], total_ends.at[low], tend_send.at[low], tend_recv.at[low], me
        ).wait_recv()
        return c

    lax.fori_loop(0, z, take_totals, 0)

    def enter(u, carry):
        at = pl.ds(pl.multiple_of(u * DH, DH), DH)
        row = pl.ds(j * per + u, 1)

        def add(low, run):
            return run * jnp.exp(total_ends[low, row, :]) + totals[low, at, :].astype(F32)

        start = lax.fori_loop(0, z, add, jnp.zeros((DH, DH), F32))
        past = jnp.zeros((1, DH), F32)
        for c in range(PLANE):
            outgoing[c, at, :] = (prefix[c, at, :] + start * jnp.exp(past)).astype(BF16)
            past = past + ends[c, row, :]
        return carry

    lax.fori_loop(0, per, enter, 0)

    def state_copy(o):
        c = lax.rem(j + o, PLANE)
        return remote(outgoing.at[c], state.at[j], st_send.at[c], st_recv.at[j], base + c)

    for o in range(1, PLANE):
        state_copy(o).start()
    state[j] = outgoing[j]

    @pl.when(z > 0)
    def _():
        forward_row(0, False)

    def lower(r, c):
        @pl.when(r + 1 < z)
        def _():
            forward_row(r + 1, False)

        for k2 in range(CHIPS):
            s = r * PLANE + k2 * 2 + (1 - core)
            kv_copy(s, sib_send.at[r, 0], me).wait_recv()
        for kh in range(KVH):
            fold(r, kh, False)
        return c

    lax.fori_loop(0, z, lower, 0)
    for kh in range(KVH):
        out = (acc_ref[kh] / den_ref[kh]).T
        for g in range(group):
            h = kh * group + g
            soft_out[:, h * DH : (h + 1) * DH] = out[g * tok : (g + 1) * tok, :].astype(BF16)

    for o in range(1, PLANE):
        c = lax.rem(j + o, PLANE)
        remote(outgoing.at[c], state.at[c], st_send.at[c], st_recv.at[c], me).wait_recv()

    def finish(g, c):
        for u in range(per):
            h = g * per + u
            cols = columns(h)
            inter = dot(q_lin[:, cols], state[g, u * DH : (u + 1) * DH, :], ((1,), (0,)))
            full = inter * jnp.exp(column_of(h)) + mixed[:, cols]
            mean = jnp.mean(full * full, axis=1, keepdims=True)
            lin_out[:, cols] = (full / jnp.sqrt(mean + 1e-6)).astype(BF16)
        return c

    lax.fori_loop(0, PLANE, finish, 0)

    column_all(True)
    own_row(True)
    forward_own(True)

    def drain_rows(r, c):
        lower_row(r, True)
        forward_row(r, True)
        return c

    lax.fori_loop(0, z, drain_rows, 0)

    def drain_totals(up, c):
        for copy in total_copies(up):
            copy.wait_send()
        return c

    lax.fori_loop(z + 1, planes, drain_totals, 0)
    for o in range(1, PLANE):
        end_copy(o).wait_send()
        sum_copy(o).wait_send()
        state_copy(o).wait_send()


def per_device(n, *args):
    q_lin, k_lin, v_lin, log_decay, pattern, q_soft, k_soft, v_soft = args
    tok, heads = log_decay.shape
    kvw = k_soft.shape[1]
    planes = n // PLANE
    share = heads // PLANE * DH
    rows = HQ // KVH * tok
    dma = pltpu.SemaphoreType.DMA
    vmem = pl.BlockSpec(memory_space=pltpu.VMEM)
    return pl.pallas_call(
        functools.partial(kernel, planes),
        out_shape=(
            jax.ShapeDtypeStruct(q_lin.shape, BF16),
            jax.ShapeDtypeStruct(q_soft.shape, BF16),
        ),
        in_specs=[vmem] * 8,
        out_specs=(vmem, vmem),
        scratch_shapes=[
            pltpu.VMEM((n, tok, 2 * kvw), BF16),
            pltpu.VMEM((PLANE, heads, DH), F32),
            pltpu.VMEM((PLANE, share, DH), BF16),
            pltpu.VMEM((PLANE, share, DH), BF16),
            pltpu.VMEM((planes, share, DH), BF16),
            pltpu.VMEM((planes, heads, DH), F32),
            pltpu.VMEM((PLANE, share, DH), F32),
            pltpu.VMEM((PLANE, share, DH), BF16),
            pltpu.VMEM((PLANE, share, DH), BF16),
            pltpu.VMEM((tok, heads * DH), F32),
            pltpu.VMEM((tok, heads), F32),
            pltpu.VMEM((heads, tok), F32),
            pltpu.VMEM((KVH, rows, DH), BF16),
            pltpu.VMEM((KVH, 1, rows), F32),
            pltpu.VMEM((KVH, 1, rows), F32),
            pltpu.VMEM((KVH, DH, rows), F32),
            dma((n,)),
            dma((planes,)),
            dma((planes, CHIPS - 1)),
            dma((planes, CHIPS)),
            dma((PLANE,)),
            dma((PLANE,)),
            dma((PLANE,)),
            dma((PLANE,)),
            dma((planes,)),
            dma((planes,)),
            dma((planes,)),
            dma((planes,)),
            dma((PLANE,)),
            dma((PLANE,)),
        ],
        compiler_params=pltpu.CompilerParams(
            collective_id=0, has_side_effects=True, vmem_limit_bytes=48 * 1024 * 1024
        ),
        name="both_layers",
    )(*args)


def solution(mesh):
    spec = P(("parts", "ctx"), None)
    return jax.shard_map(
        functools.partial(per_device, mesh.shape["ctx"]),
        mesh=mesh,
        in_specs=(spec,) * 8,
        out_specs=(spec, spec),
        check_vma=False,
    )
```

```python
import functools
import math

import jax
import jax.numpy as jnp
from jax import lax
from jax.experimental import pallas as pl
from jax.experimental.pallas import tpu as pltpu
from jax.sharding import PartitionSpec as P

DH = 128
HQ = 32
KVH = 4
PLANE = 8
CHIPS = 4
NEG = -1e30
F32 = jnp.float32
BF16 = jnp.bfloat16


def dot(a, b, dims, precision=None):
    return lax.dot_general(
        a, b, (dims, ((), ())), precision=precision, preferred_element_type=F32
    )


def kernel(
    planes,
    q_lin_hbm,
    k_lin_hbm,
    v_lin_hbm,
    log_decay,
    pattern,
    q_soft_hbm,
    k_soft_hbm,
    v_soft_hbm,
    lin_out,
    soft_out,
    q_lin,
    k_lin,
    v_lin,
    q_soft,
    kv,
    ends,
    sums,
    theirs,
    chip_sums,
    gathered,
    prefix,
    plane_sum,
    carry_in,
    carry_out,
    outgoing,
    entry,
    handed,
    state,
    mixed,
    ell_ref,
    ell_rows,
    queries,
    top_ref,
    den_ref,
    acc_ref,
    load,
    kv_recv,
    col_send,
    in_send,
    sib_send,
    end_send,
    end_recv,
    swap_send,
    swap_recv,
    sum_send,
    sum_recv,
    up_send,
    up_recv,
    out_send,
    out_recv,
    hand_send,
    hand_recv,
):
    tok = q_lin.shape[0]
    heads = log_decay.shape[0]
    per = heads // PLANE
    blocks = pattern.shape[1]
    width = tok // blocks
    kvw = k_soft_hbm.shape[1]
    group = HQ // KVH
    rows = group * tok
    me = lax.axis_index("ctx")
    z, j = me // PLANE, lax.rem(me, PLANE)
    chip, core = j // 2, lax.rem(j, 2)
    base = z * PLANE
    sibling = base + chip * 2 + (1 - core)

    def remote(src, dst, send, recv, device):
        return pltpu.make_async_remote_copy(
            src_ref=src,
            dst_ref=dst,
            send_sem=send,
            recv_sem=recv,
            device_id={"ctx": device},
            device_id_type=pl.DeviceIdType.MESH,
        )

    def span(s):
        return kv.at[s]

    def kv_copy(s, send, device):
        return remote(span(s), span(s), send, kv_recv.at[s], device)

    def other_chip(o):
        return lax.rem(chip + o, CHIPS)

    loads = [
        pltpu.make_async_copy(src, dst, load.at[i])
        for i, (src, dst) in enumerate(
            (
                (k_soft_hbm, kv.at[me, :, pl.ds(0, kvw)]),
                (v_soft_hbm, kv.at[me, :, pl.ds(kvw, kvw)]),
                (k_lin_hbm, k_lin),
                (v_lin_hbm, v_lin),
                (q_lin_hbm, q_lin),
                (q_soft_hbm, q_soft),
            )
        )
    ]
    for copy in loads:
        copy.start()
    for p in range(PLANE):
        @pl.when(p > j)
        def _():
            kv[base + p] = jnp.zeros((tok, 2 * kvw), BF16)

    barrier = pltpu.get_barrier_semaphore()
    for o in range(1, PLANE):
        pl.semaphore_signal(
            barrier, inc=1, device_id={"ctx": base + lax.rem(j + o, PLANE)},
            device_id_type=pl.DeviceIdType.MESH,
        )
    for o in range(1, planes):
        pl.semaphore_signal(
            barrier, inc=1, device_id={"ctx": lax.rem(z + o, planes) * PLANE + j},
            device_id_type=pl.DeviceIdType.MESH,
        )
    pl.semaphore_wait(barrier, PLANE - 1 + planes - 1)

    def column(up, wait):
        copy = kv_copy(me, col_send.at[up], up * PLANE + j)
        copy.wait_send() if wait else copy.start()

    def column_all(wait):
        def body(up, c):
            column(up, wait)
            return c

        lax.fori_loop(z + 1, planes, body, 0)

    def own_row(wait):
        for o in range(1, CHIPS):
            k2 = other_chip(o)

            @pl.when(k2 > chip)
            def _():
                copy = kv_copy(me, in_send.at[z, o - 1], base + k2 * 2 + core)
                copy.wait_send() if wait else copy.start()

        @pl.when(core == 0)
        def _():
            copy = kv_copy(me, sib_send.at[z, 0], sibling)
            copy.wait_send() if wait else copy.start()

    def lower_row(r, wait):
        s = r * PLANE + j
        if not wait:
            kv_copy(s, col_send.at[r], me).wait_recv()
        for o in range(1, CHIPS):
            copy = kv_copy(s, in_send.at[r, o - 1], base + other_chip(o) * 2 + core)
            copy.wait_send() if wait else copy.start()
        copy = kv_copy(s, sib_send.at[r, 0], sibling)
        copy.wait_send() if wait else copy.start()

    def forward_row(r, wait):
        for o in range(1, CHIPS):
            s = r * PLANE + other_chip(o) * 2 + core
            if not wait:
                kv_copy(s, sib_send.at[r, o], sibling).wait_recv()
            copy = kv_copy(s, sib_send.at[r, o], sibling)
            copy.wait_send() if wait else copy.start()

    def forward_own(wait):
        for o in range(1, CHIPS):
            k2 = other_chip(o)

            @pl.when(k2 < chip)
            def _():
                s = base + k2 * 2 + core
                copy = kv_copy(s, sib_send.at[z, o], sibling)
                if not wait:
                    copy.wait_recv()
                copy.wait_send() if wait else copy.start()

    loads[0].wait()
    loads[1].wait()
    column_all(False)
    own_row(False)

    t_pos = lax.broadcasted_iota(jnp.int32, (tok, tok), 0)
    s_pos = lax.broadcasted_iota(jnp.int32, (tok, tok), 1)
    causal = s_pos <= t_pos
    tri = causal.astype(F32)
    high = lax.Precision.HIGHEST
    decay = log_decay[...]
    ell_ref[...] = dot(tri, decay, ((1,), (1,)), high)
    ell_rows[...] = dot(decay, tri, ((1,), (1,)), high)
    ends[j] = dot(decay, jnp.ones((tok, DH), F32), ((1,), (0,)), high)

    def end_copy(o):
        return remote(
            ends.at[j], ends.at[j], end_send.at[o], end_recv.at[j],
            base + lax.rem(j + o, PLANE),
        )

    for o in range(1, PLANE):
        end_copy(o).start()

    lane = lax.broadcasted_iota(jnp.int32, (tok, heads), 1)

    def column_of(h):
        return jnp.sum(jnp.where(lane == h, ell_ref[...], 0.0), axis=1, keepdims=True)

    def columns(h):
        return pl.ds(pl.multiple_of(h * DH, DH), DH)

    def head_of(u, c2, k2):
        return (2 * k2 + c2) * per + u

    def swap_copy(u):
        return remote(
            sums.at[u, 1 - core], theirs.at[u], swap_send.at[u], swap_recv.at[u], sibling
        )

    def summarize(u, carry):
        for half in range(2):
            c2 = (1 - core) if half == 0 else core
            for k2 in range(CHIPS):
                h = head_of(u, c2, k2)
                col = column_of(h)
                scaled = k_lin[:, columns(h)].astype(F32) * jnp.exp(col[tok - 1 : tok, :] - col)
                total = dot(scaled.astype(BF16), v_lin[:, columns(h)], ((0,), (0,)))
                sums[u, c2, k2] = total.astype(BF16)
            if half == 0:
                swap_copy(u).start()
        return carry

    loads[2].wait()
    loads[3].wait()
    lax.fori_loop(0, per, summarize, 0)

    def end_wait(p):
        remote(ends.at[p], ends.at[p], end_send.at[0], end_recv.at[p], me).wait_recv()

    end_wait(chip * 2 + 1 - core)
    first, second = chip * 2, chip * 2 + 1

    def sum_copy(u, o):
        k2 = other_chip(o)
        return remote(
            chip_sums.at[u, k2], gathered.at[u, chip], sum_send.at[u, k2],
            sum_recv.at[u, chip], base + k2 * 2 + core,
        )

    def early(u, k2):
        return jnp.where(core == 0, sums[u, core, k2], theirs[u, k2]).astype(F32)

    def late(u, k2):
        return jnp.where(core == 0, theirs[u, k2], sums[u, core, k2]).astype(F32)

    def combine(u, carry):
        swap_copy(u).wait_recv()
        for k2 in range(CHIPS):
            fade = jnp.exp(ends[second, pl.ds(head_of(u, core, k2), 1), :])
            chip_sums[u, k2] = (early(u, k2) * fade + late(u, k2)).astype(BF16)
        for o in range(1, CHIPS):
            sum_copy(u, o).start()
        gathered[u, chip] = chip_sums[u, chip]
        return carry

    lax.fori_loop(0, per, combine, 0)

    def send_lower(r, c):
        lower_row(r, False)
        return c

    lax.fori_loop(0, z, send_lower, 0)

    t_blk, s_blk = t_pos // width, s_pos // width
    live = t_blk == s_blk
    for b in range(blocks):
        for a in range(b):
            live = live | (
                (t_blk == b) & (s_blk == a) & (pattern[b : b + 1, a : a + 1] == 1)
            )
    live = live & causal

    def within(g, c):
        for u in range(per):
            h = g * per + u
            cols = columns(h)
            scores = dot(q_lin[:, cols], k_lin[:, cols], ((1,), (1,)))
            diff = column_of(h) - ell_rows[pl.ds(h, 1), :]
            weight = jnp.where(live, scores * jnp.exp(jnp.where(live, diff, 0.0)), 0.0)
            mixed[:, cols] = dot(weight.astype(BF16), v_lin[:, cols], ((1,), (0,)))
        return c

    loads[4].wait()
    lax.fori_loop(0, PLANE, within, 0)

    loads[5].wait()
    for kh in range(KVH):
        for g in range(group):
            h = kh * group + g
            queries[kh, g * tok : (g + 1) * tok, :] = q_soft[:, h * DH : (h + 1) * DH]

    for o in range(1, PLANE):
        p = lax.rem(j + o, PLANE)

        @pl.when(p != chip * 2 + 1 - core)
        def _():
            end_wait(p)

    def chip_end(k2, row):
        return ends[2 * k2, row, :] + ends[2 * k2 + 1, row, :]

    def scan(u, carry):
        for o in range(1, CHIPS):
            k2 = other_chip(o)
            remote(
                chip_sums.at[u, k2], gathered.at[u, k2], sum_send.at[u, k2],
                sum_recv.at[u, k2], me,
            ).wait_recv()
        row = pl.ds(j * per + u, 1)
        run = jnp.zeros((DH, DH), F32)
        for k2 in range(CHIPS):
            prefix[u, k2] = run
            run = run * jnp.exp(chip_end(k2, row)) + gathered[u, k2].astype(F32)
        plane_sum[u] = run

        @pl.when(z == 0)
        def _():
            carry_in[u] = jnp.zeros((DH, DH), BF16)
            carry_out[u] = run.astype(BF16)
            if planes > 1:
                up_copy(u).start()

        return carry

    def up_copy(u):
        return remote(
            carry_out.at[u], carry_in.at[u], up_send.at[u], up_recv.at[u], me + PLANE
        )

    lax.fori_loop(0, per, scan, 0)

    def out_copy(u, o):
        k2 = other_chip(o)
        return remote(
            outgoing.at[u, k2], entry.at[u, chip], out_send.at[u, k2],
            out_recv.at[u, chip], base + k2 * 2 + core,
        )

    def enter(u, carry):
        row = pl.ds(j * per + u, 1)

        @pl.when(z > 0)
        def _():
            up_copy(u).wait_recv()

        start = carry_in[u].astype(F32)

        @pl.when((z > 0) & (z < planes - 1))
        def _():
            whole = chip_end(0, row)
            for k2 in range(1, CHIPS):
                whole = whole + chip_end(k2, row)
            carry_out[u] = (start * jnp.exp(whole) + plane_sum[u]).astype(BF16)
            up_copy(u).start()

        past = jnp.zeros((1, DH), F32)
        for k2 in range(CHIPS):
            outgoing[u, k2] = (prefix[u, k2] + start * jnp.exp(past)).astype(BF16)
            past = past + chip_end(k2, row)
        for o in range(1, CHIPS):
            out_copy(u, o).start()
        entry[u, chip] = outgoing[u, chip]
        return carry

    lax.fori_loop(0, per, enter, 0)

    factor = math.log2(math.e) / math.sqrt(DH)

    def fold(r, kh, first):
        at = pl.ds(pl.multiple_of(r * PLANE, PLANE), PLANE)
        keys = kv[at, :, kh * DH : (kh + 1) * DH].reshape(PLANE * tok, DH)
        values = kv[at, :, kvw + kh * DH : kvw + (kh + 1) * DH].reshape(PLANE * tok, DH)
        scores = dot(keys, queries[kh], ((1,), (1,)))
        if first:
            shape = (PLANE * tok, tok)
            key = lax.broadcasted_iota(jnp.int32, shape, 0)
            query = j * tok + lax.broadcasted_iota(jnp.int32, shape, 1)
            bias = jnp.where(key <= query, 0.0, NEG)
            scores = scores + jnp.concatenate([bias] * group, axis=1)
            top = jnp.max(scores, axis=0, keepdims=True)
        else:
            old = top_ref[kh]
            top = jnp.maximum(old, jnp.max(scores, axis=0, keepdims=True))
        probs = jnp.exp2(scores * factor - top * factor)
        den = jnp.sum(probs, axis=0, keepdims=True)
        acc = dot(values, probs.astype(BF16), ((0,), (0,)))
        if not first:
            shrink = jnp.exp2((old - top) * factor)
            den = den + den_ref[kh] * shrink
            acc = acc + acc_ref[kh] * shrink
        top_ref[kh] = top
        den_ref[kh] = den
        acc_ref[kh] = acc

    forward_own(False)
    for k2 in range(CHIPS):
        @pl.when((k2 < chip) | ((k2 == chip) & (core == 1)))
        def _():
            s = base + k2 * 2 + (1 - core)
            kv_copy(s, sib_send.at[z, 0], me).wait_recv()

    for kh in range(KVH):
        fold(z, kh, True)

    def hand_copy(u):
        return remote(handed.at[u], state.at[u, core], hand_send.at[u], hand_recv.at[u], sibling)

    def hand(u, carry):
        for o in range(1, CHIPS):
            k2 = other_chip(o)
            remote(
                outgoing.at[u, k2], entry.at[u, k2], out_send.at[u, k2], out_recv.at[u, k2], me
            ).wait_recv()
        for k2 in range(CHIPS):
            fade = jnp.exp(ends[first, pl.ds(head_of(u, core, k2), 1), :])
            chip_state = entry[u, k2].astype(F32)
            later = chip_state * fade + early(u, k2)
            state[u, core, k2] = jnp.where(core == 0, chip_state, later).astype(BF16)
            handed[u, k2] = jnp.where(core == 0, later, chip_state).astype(BF16)
        hand_copy(u).start()
        return carry

    lax.fori_loop(0, per, hand, 0)

    @pl.when(z > 0)
    def _():
        forward_row(0, False)

    def lower(r, c):
        @pl.when(r + 1 < z)
        def _():
            forward_row(r + 1, False)

        for k2 in range(CHIPS):
            s = r * PLANE + k2 * 2 + (1 - core)
            kv_copy(s, sib_send.at[r, 0], me).wait_recv()
        for kh in range(KVH):
            fold(r, kh, False)
        return c

    lax.fori_loop(0, z, lower, 0)
    for kh in range(KVH):
        out = (acc_ref[kh] / den_ref[kh]).T
        for g in range(group):
            h = kh * group + g
            soft_out[:, h * DH : (h + 1) * DH] = out[g * tok : (g + 1) * tok, :].astype(BF16)

    def await_hand(u, c):
        remote(
            handed.at[u], state.at[u, 1 - core], hand_send.at[u], hand_recv.at[u], me
        ).wait_recv()
        return c

    lax.fori_loop(0, per, await_hand, 0)

    def finish(u, c):
        for c2 in range(2):
            for k2 in range(CHIPS):
                h = head_of(u, c2, k2)
                cols = columns(h)
                inter = dot(q_lin[:, cols], state[u, c2, k2], ((1,), (0,)))
                full = inter * jnp.exp(column_of(h)) + mixed[:, cols]
                mean = jnp.mean(full * full, axis=1, keepdims=True)
                lin_out[:, cols] = (full / jnp.sqrt(mean + 1e-6)).astype(BF16)
        return c

    lax.fori_loop(0, per, finish, 0)

    column_all(True)
    own_row(True)
    forward_own(True)

    def drain_rows(r, c):
        lower_row(r, True)
        forward_row(r, True)
        return c

    lax.fori_loop(0, z, drain_rows, 0)

    for o in range(1, PLANE):
        end_copy(o).wait_send()

    def drain(u, c):
        swap_copy(u).wait_send()
        hand_copy(u).wait_send()
        for o in range(1, CHIPS):
            sum_copy(u, o).wait_send()
            out_copy(u, o).wait_send()

        @pl.when(z < planes - 1)
        def _():
            up_copy(u).wait_send()

        return c

    lax.fori_loop(0, per, drain, 0)


def per_device(n, *args):
    q_lin, k_lin, v_lin, log_decay, pattern, q_soft, k_soft, v_soft = args
    tok, heads = log_decay.shape
    kvw = k_soft.shape[1]
    planes = n // PLANE
    per = heads // PLANE
    rows = HQ // KVH * tok
    dma = pltpu.SemaphoreType.DMA
    vmem = pl.BlockSpec(memory_space=pltpu.VMEM)
    hbm = pl.BlockSpec(memory_space=pltpu.HBM)
    return pl.pallas_call(
        functools.partial(kernel, planes),
        out_shape=(
            jax.ShapeDtypeStruct(q_lin.shape, BF16),
            jax.ShapeDtypeStruct(q_soft.shape, BF16),
        ),
        in_specs=[hbm] * 3 + [vmem] * 2 + [hbm] * 3,
        out_specs=(vmem, vmem),
        scratch_shapes=[
            pltpu.VMEM(q_lin.shape, BF16),
            pltpu.VMEM(q_lin.shape, BF16),
            pltpu.VMEM(q_lin.shape, BF16),
            pltpu.VMEM(q_soft.shape, BF16),
            pltpu.VMEM((n, tok, 2 * kvw), BF16),
            pltpu.VMEM((PLANE, heads, DH), F32),
            pltpu.VMEM((per, 2, CHIPS, DH, DH), BF16),
            pltpu.VMEM((per, CHIPS, DH, DH), BF16),
            pltpu.VMEM((per, CHIPS, DH, DH), BF16),
            pltpu.VMEM((per, CHIPS, DH, DH), BF16),
            pltpu.VMEM((per, CHIPS, DH, DH), F32),
            pltpu.VMEM((per, DH, DH), F32),
            pltpu.VMEM((per, DH, DH), BF16),
            pltpu.VMEM((per, DH, DH), BF16),
            pltpu.VMEM((per, CHIPS, DH, DH), BF16),
            pltpu.VMEM((per, CHIPS, DH, DH), BF16),
            pltpu.VMEM((per, CHIPS, DH, DH), BF16),
            pltpu.VMEM((per, 2, CHIPS, DH, DH), BF16),
            pltpu.VMEM((tok, heads * DH), F32),
            pltpu.VMEM((tok, heads), F32),
            pltpu.VMEM((heads, tok), F32),
            pltpu.VMEM((KVH, rows, DH), BF16),
            pltpu.VMEM((KVH, 1, rows), F32),
            pltpu.VMEM((KVH, 1, rows), F32),
            pltpu.VMEM((KVH, DH, rows), F32),
            dma((6,)),
            dma((n,)),
            dma((planes,)),
            dma((planes, CHIPS - 1)),
            dma((planes, CHIPS)),
            dma((PLANE,)),
            dma((PLANE,)),
            dma((per,)),
            dma((per,)),
            dma((per, CHIPS)),
            dma((per, CHIPS)),
            dma((per,)),
            dma((per,)),
            dma((per, CHIPS)),
            dma((per, CHIPS)),
            dma((per,)),
            dma((per,)),
        ],
        compiler_params=pltpu.CompilerParams(
            collective_id=0, has_side_effects=True, vmem_limit_bytes=60 * 1024 * 1024
        ),
        name="both_layers",
    )(q_lin, k_lin, v_lin, log_decay.T, pattern, q_soft, k_soft, v_soft)


def solution(mesh):
    spec = P(("parts", "ctx"), None)
    return jax.shard_map(
        functools.partial(per_device, mesh.shape["ctx"]),
        mesh=mesh,
        in_specs=(spec,) * 8,
        out_specs=(spec, spec),
        check_vma=False,
    )
```

```python
import functools
import math

import jax
import jax.numpy as jnp
from jax import lax
from jax.experimental import pallas as pl
from jax.experimental.pallas import tpu as pltpu
from jax.sharding import PartitionSpec as P

DH = 128
HQ = 32
KVH = 4
PLANE = 8
CHIPS = 4
NEG = -1e30
F32 = jnp.float32
BF16 = jnp.bfloat16


def dot(a, b, dims, precision=None):
    return lax.dot_general(
        a, b, (dims, ((), ())), precision=precision, preferred_element_type=F32
    )


def kernel(
    planes,
    q_lin_hbm,
    k_lin_hbm,
    v_lin_hbm,
    log_decay,
    pattern,
    q_soft_hbm,
    k_soft_hbm,
    v_soft_hbm,
    lin_out,
    soft_out,
    q_lin,
    k_lin,
    v_lin,
    q_soft,
    kv,
    ends,
    sums,
    theirs,
    chip_sums,
    gathered,
    prefix,
    plane_sum,
    carry_in,
    carry_out,
    outgoing,
    entry,
    handed,
    state,
    mixed,
    ell_ref,
    ell_rows,
    queries,
    top_ref,
    den_ref,
    acc_ref,
    load,
    kv_recv,
    col_send,
    in_send,
    sib_send,
    end_send,
    end_recv,
    swap_send,
    swap_recv,
    sum_send,
    sum_recv,
    up_send,
    up_recv,
    out_send,
    out_recv,
    hand_send,
    hand_recv,
):
    tok = q_lin.shape[0]
    heads = log_decay.shape[0]
    per = heads // PLANE
    blocks = pattern.shape[1]
    width = tok // blocks
    kvw = k_soft_hbm.shape[1]
    group = HQ // KVH
    rows = group * tok
    me = lax.axis_index("ctx")
    z, j = me // PLANE, lax.rem(me, PLANE)
    chip, core = j // 2, lax.rem(j, 2)
    base = z * PLANE
    sibling = base + chip * 2 + (1 - core)

    def remote(src, dst, send, recv, device):
        return pltpu.make_async_remote_copy(
            src_ref=src,
            dst_ref=dst,
            send_sem=send,
            recv_sem=recv,
            device_id={"ctx": device},
            device_id_type=pl.DeviceIdType.MESH,
        )

    def span(s):
        return kv.at[s]

    def kv_copy(s, send, device):
        return remote(span(s), span(s), send, kv_recv.at[s], device)

    def other_chip(o):
        return lax.rem(chip + o, CHIPS)

    loads = [
        pltpu.make_async_copy(src, dst, load.at[i])
        for i, (src, dst) in enumerate(
            (
                (k_soft_hbm, kv.at[me, :, pl.ds(0, kvw)]),
                (v_soft_hbm, kv.at[me, :, pl.ds(kvw, kvw)]),
                (k_lin_hbm, k_lin),
                (v_lin_hbm, v_lin),
                (q_lin_hbm, q_lin),
                (q_soft_hbm, q_soft),
            )
        )
    ]
    for copy in loads:
        copy.start()
    for p in range(PLANE):
        @pl.when(p > j)
        def _():
            kv[base + p] = jnp.zeros((tok, 2 * kvw), BF16)

    barrier = pltpu.get_barrier_semaphore()
    for o in range(1, PLANE):
        pl.semaphore_signal(
            barrier, inc=1, device_id={"ctx": base + lax.rem(j + o, PLANE)},
            device_id_type=pl.DeviceIdType.MESH,
        )
    for o in range(1, planes):
        pl.semaphore_signal(
            barrier, inc=1, device_id={"ctx": lax.rem(z + o, planes) * PLANE + j},
            device_id_type=pl.DeviceIdType.MESH,
        )
    pl.semaphore_wait(barrier, PLANE - 1 + planes - 1)

    def column(up, wait):
        copy = kv_copy(me, col_send.at[up], up * PLANE + j)
        copy.wait_send() if wait else copy.start()

    def column_all(wait):
        def body(i, c):
            column(planes + z - i, wait)
            return c

        lax.fori_loop(z + 1, planes, body, 0)

    def own_row(wait):
        for o in range(1, CHIPS):
            k2 = other_chip(o)

            @pl.when(k2 > chip)
            def _():
                copy = kv_copy(me, in_send.at[z, o - 1], base + k2 * 2 + core)
                copy.wait_send() if wait else copy.start()

        @pl.when(core == 0)
        def _():
            copy = kv_copy(me, sib_send.at[z, 0], sibling)
            copy.wait_send() if wait else copy.start()

    def lower_row(r, wait):
        s = r * PLANE + j
        if not wait:
            kv_copy(s, col_send.at[r], me).wait_recv()
        for o in range(1, CHIPS):
            copy = kv_copy(s, in_send.at[r, o - 1], base + other_chip(o) * 2 + core)
            copy.wait_send() if wait else copy.start()
        copy = kv_copy(s, sib_send.at[r, 0], sibling)
        copy.wait_send() if wait else copy.start()

    def forward_row(r, wait):
        for o in range(1, CHIPS):
            s = r * PLANE + other_chip(o) * 2 + core
            if not wait:
                kv_copy(s, sib_send.at[r, o], sibling).wait_recv()
            copy = kv_copy(s, sib_send.at[r, o], sibling)
            copy.wait_send() if wait else copy.start()

    def forward_own(wait):
        for o in range(1, CHIPS):
            k2 = other_chip(o)

            @pl.when(k2 < chip)
            def _():
                s = base + k2 * 2 + core
                copy = kv_copy(s, sib_send.at[z, o], sibling)
                if not wait:
                    copy.wait_recv()
                copy.wait_send() if wait else copy.start()

    loads[0].wait()
    loads[1].wait()
    column_all(False)
    own_row(False)

    t_pos = lax.broadcasted_iota(jnp.int32, (tok, tok), 0)
    s_pos = lax.broadcasted_iota(jnp.int32, (tok, tok), 1)
    causal = s_pos <= t_pos
    tri = causal.astype(F32)
    high = lax.Precision.HIGHEST
    decay = log_decay[...]
    ell_ref[...] = dot(tri, decay, ((1,), (1,)), high)
    ell_rows[...] = dot(decay, tri, ((1,), (1,)), high)
    ends[j] = dot(decay, jnp.ones((tok, DH), F32), ((1,), (0,)), high)

    def end_copy(o):
        return remote(
            ends.at[j], ends.at[j], end_send.at[o], end_recv.at[j],
            base + lax.rem(j + o, PLANE),
        )

    for o in range(1, PLANE):
        end_copy(o).start()

    lane = lax.broadcasted_iota(jnp.int32, (tok, heads), 1)

    def column_of(h):
        return jnp.sum(jnp.where(lane == h, ell_ref[...], 0.0), axis=1, keepdims=True)

    def columns(h):
        return pl.ds(pl.multiple_of(h * DH, DH), DH)

    def head_of(u, c2, k2):
        return (2 * k2 + c2) * per + u

    def swap_copy(u):
        return remote(
            sums.at[u, 1 - core], theirs.at[u], swap_send.at[u], swap_recv.at[u], sibling
        )

    def summarize(u, carry):
        for half in range(2):
            c2 = (1 - core) if half == 0 else core
            for k2 in range(CHIPS):
                h = head_of(u, c2, k2)
                col = column_of(h)
                scaled = k_lin[:, columns(h)].astype(F32) * jnp.exp(col[tok - 1 : tok, :] - col)
                total = dot(scaled.astype(BF16), v_lin[:, columns(h)], ((0,), (0,)))
                sums[u, c2, k2] = total.astype(BF16)
            if half == 0:
                swap_copy(u).start()
        return carry

    loads[2].wait()
    loads[3].wait()
    lax.fori_loop(0, per, summarize, 0)

    def end_wait(p):
        remote(ends.at[p], ends.at[p], end_send.at[0], end_recv.at[p], me).wait_recv()

    end_wait(chip * 2 + 1 - core)
    first, second = chip * 2, chip * 2 + 1

    def sum_copy(u, o):
        k2 = other_chip(o)
        return remote(
            chip_sums.at[u, k2], gathered.at[u, chip], sum_send.at[u, k2],
            sum_recv.at[u, chip], base + k2 * 2 + core,
        )

    def early(u, k2):
        return jnp.where(core == 0, sums[u, core, k2], theirs[u, k2]).astype(F32)

    def late(u, k2):
        return jnp.where(core == 0, theirs[u, k2], sums[u, core, k2]).astype(F32)

    def combine(u, carry):
        swap_copy(u).wait_recv()
        for k2 in range(CHIPS):
            fade = jnp.exp(ends[second, pl.ds(head_of(u, core, k2), 1), :])
            chip_sums[u, k2] = (early(u, k2) * fade + late(u, k2)).astype(BF16)
        for o in range(1, CHIPS):
            sum_copy(u, o).start()
        gathered[u, chip] = chip_sums[u, chip]
        return carry

    lax.fori_loop(0, per, combine, 0)

    def send_lower(r, c):
        lower_row(z - 1 - r, False)
        return c

    lax.fori_loop(0, z, send_lower, 0)

    t_blk, s_blk = t_pos // width, s_pos // width
    live = t_blk == s_blk
    for b in range(blocks):
        for a in range(b):
            live = live | (
                (t_blk == b) & (s_blk == a) & (pattern[b : b + 1, a : a + 1] == 1)
            )
    live = live & causal

    def within(g, c):
        for u in range(per):
            h = g * per + u
            cols = columns(h)
            scores = dot(q_lin[:, cols], k_lin[:, cols], ((1,), (1,)))
            diff = column_of(h) - ell_rows[pl.ds(h, 1), :]
            weight = jnp.where(live, scores * jnp.exp(jnp.where(live, diff, 0.0)), 0.0)
            mixed[:, cols] = dot(weight.astype(BF16), v_lin[:, cols], ((1,), (0,)))
        return c

    loads[4].wait()
    lax.fori_loop(0, PLANE, within, 0)

    loads[5].wait()
    for kh in range(KVH):
        for g in range(group):
            h = kh * group + g
            queries[kh, g * tok : (g + 1) * tok, :] = q_soft[:, h * DH : (h + 1) * DH]

    for o in range(1, PLANE):
        p = lax.rem(j + o, PLANE)

        @pl.when(p != chip * 2 + 1 - core)
        def _():
            end_wait(p)

    def chip_end(k2, row):
        return ends[2 * k2, row, :] + ends[2 * k2 + 1, row, :]

    def scan(u, carry):
        for o in range(1, CHIPS):
            k2 = other_chip(o)
            remote(
                chip_sums.at[u, k2], gathered.at[u, k2], sum_send.at[u, k2],
                sum_recv.at[u, k2], me,
            ).wait_recv()
        row = pl.ds(j * per + u, 1)
        run = jnp.zeros((DH, DH), F32)
        for k2 in range(CHIPS):
            prefix[u, k2] = run
            run = run * jnp.exp(chip_end(k2, row)) + gathered[u, k2].astype(F32)
        plane_sum[u] = run

        @pl.when(z == 0)
        def _():
            carry_in[u] = jnp.zeros((DH, DH), BF16)
            carry_out[u] = run.astype(BF16)
            if planes > 1:
                up_copy(u).start()

        return carry

    def up_copy(u):
        return remote(
            carry_out.at[u], carry_in.at[u], up_send.at[u], up_recv.at[u], me + PLANE
        )

    lax.fori_loop(0, per, scan, 0)

    def out_copy(u, o):
        k2 = other_chip(o)
        return remote(
            outgoing.at[u, k2], entry.at[u, chip], out_send.at[u, k2],
            out_recv.at[u, chip], base + k2 * 2 + core,
        )

    def enter(u, carry):
        row = pl.ds(j * per + u, 1)

        @pl.when(z > 0)
        def _():
            up_copy(u).wait_recv()

        start = carry_in[u].astype(F32)

        @pl.when((z > 0) & (z < planes - 1))
        def _():
            whole = chip_end(0, row)
            for k2 in range(1, CHIPS):
                whole = whole + chip_end(k2, row)
            carry_out[u] = (start * jnp.exp(whole) + plane_sum[u]).astype(BF16)
            up_copy(u).start()

        past = jnp.zeros((1, DH), F32)
        for k2 in range(CHIPS):
            outgoing[u, k2] = (prefix[u, k2] + start * jnp.exp(past)).astype(BF16)
            past = past + chip_end(k2, row)
        for o in range(1, CHIPS):
            out_copy(u, o).start()
        entry[u, chip] = outgoing[u, chip]
        return carry

    lax.fori_loop(0, per, enter, 0)

    factor = math.log2(math.e) / math.sqrt(DH)

    def fold(r, kh, first):
        at = pl.ds(pl.multiple_of(r * PLANE, PLANE), PLANE)
        keys = kv[at, :, kh * DH : (kh + 1) * DH].reshape(PLANE * tok, DH)
        values = kv[at, :, kvw + kh * DH : kvw + (kh + 1) * DH].reshape(PLANE * tok, DH)
        scores = dot(keys, queries[kh], ((1,), (1,)))
        if first:
            shape = (PLANE * tok, tok)
            key = lax.broadcasted_iota(jnp.int32, shape, 0)
            query = j * tok + lax.broadcasted_iota(jnp.int32, shape, 1)
            bias = jnp.where(key <= query, 0.0, NEG)
            scores = scores + jnp.concatenate([bias] * group, axis=1)
            top = jnp.max(scores, axis=0, keepdims=True)
        else:
            old = top_ref[kh]
            top = jnp.maximum(old, jnp.max(scores, axis=0, keepdims=True))
        probs = jnp.exp2(scores * factor - top * factor)
        den = jnp.sum(probs, axis=0, keepdims=True)
        acc = dot(values, probs.astype(BF16), ((0,), (0,)))
        if not first:
            shrink = jnp.exp2((old - top) * factor)
            den = den + den_ref[kh] * shrink
            acc = acc + acc_ref[kh] * shrink
        top_ref[kh] = top
        den_ref[kh] = den
        acc_ref[kh] = acc

    forward_own(False)
    for k2 in range(CHIPS):
        @pl.when((k2 < chip) | ((k2 == chip) & (core == 1)))
        def _():
            s = base + k2 * 2 + (1 - core)
            kv_copy(s, sib_send.at[z, 0], me).wait_recv()

    for kh in range(KVH):
        fold(z, kh, True)

    def hand_copy(u):
        return remote(handed.at[u], state.at[u, core], hand_send.at[u], hand_recv.at[u], sibling)

    def hand(u, carry):
        for o in range(1, CHIPS):
            k2 = other_chip(o)
            remote(
                outgoing.at[u, k2], entry.at[u, k2], out_send.at[u, k2], out_recv.at[u, k2], me
            ).wait_recv()
        for k2 in range(CHIPS):
            fade = jnp.exp(ends[first, pl.ds(head_of(u, core, k2), 1), :])
            chip_state = entry[u, k2].astype(F32)
            later = chip_state * fade + early(u, k2)
            state[u, core, k2] = jnp.where(core == 0, chip_state, later).astype(BF16)
            handed[u, k2] = jnp.where(core == 0, later, chip_state).astype(BF16)
        hand_copy(u).start()
        return carry

    lax.fori_loop(0, per, hand, 0)

    @pl.when(z > 0)
    def _():
        forward_row(z - 1, False)

    def await_hand(u, c):
        remote(
            handed.at[u], state.at[u, 1 - core], hand_send.at[u], hand_recv.at[u], me
        ).wait_recv()
        return c

    lax.fori_loop(0, per, await_hand, 0)

    def finish(u, c):
        for c2 in range(2):
            for k2 in range(CHIPS):
                h = head_of(u, c2, k2)
                cols = columns(h)
                inter = dot(q_lin[:, cols], state[u, c2, k2], ((1,), (0,)))
                full = inter * jnp.exp(column_of(h)) + mixed[:, cols]
                mean = jnp.mean(full * full, axis=1, keepdims=True)
                lin_out[:, cols] = (full / jnp.sqrt(mean + 1e-6)).astype(BF16)
        return c

    lax.fori_loop(0, per, finish, 0)

    def lower(i, c):
        r = z - 1 - i

        @pl.when(r > 0)
        def _():
            forward_row(r - 1, False)

        for k2 in range(CHIPS):
            s = r * PLANE + k2 * 2 + (1 - core)
            kv_copy(s, sib_send.at[r, 0], me).wait_recv()
        for kh in range(KVH):
            fold(r, kh, False)
        return c

    lax.fori_loop(0, z, lower, 0)
    for kh in range(KVH):
        out = (acc_ref[kh] / den_ref[kh]).T
        for g in range(group):
            h = kh * group + g
            soft_out[:, h * DH : (h + 1) * DH] = out[g * tok : (g + 1) * tok, :].astype(BF16)

    column_all(True)
    own_row(True)
    forward_own(True)

    def drain_rows(r, c):
        lower_row(r, True)
        forward_row(r, True)
        return c

    lax.fori_loop(0, z, drain_rows, 0)

    for o in range(1, PLANE):
        end_copy(o).wait_send()

    def drain(u, c):
        swap_copy(u).wait_send()
        hand_copy(u).wait_send()
        for o in range(1, CHIPS):
            sum_copy(u, o).wait_send()
            out_copy(u, o).wait_send()

        @pl.when(z < planes - 1)
        def _():
            up_copy(u).wait_send()

        return c

    lax.fori_loop(0, per, drain, 0)


def per_device(n, *args):
    q_lin, k_lin, v_lin, log_decay, pattern, q_soft, k_soft, v_soft = args
    tok, heads = log_decay.shape
    kvw = k_soft.shape[1]
    planes = n // PLANE
    per = heads // PLANE
    rows = HQ // KVH * tok
    dma = pltpu.SemaphoreType.DMA
    vmem = pl.BlockSpec(memory_space=pltpu.VMEM)
    hbm = pl.BlockSpec(memory_space=pltpu.HBM)
    return pl.pallas_call(
        functools.partial(kernel, planes),
        out_shape=(
            jax.ShapeDtypeStruct(q_lin.shape, BF16),
            jax.ShapeDtypeStruct(q_soft.shape, BF16),
        ),
        in_specs=[hbm] * 3 + [vmem] * 2 + [hbm] * 3,
        out_specs=(vmem, vmem),
        scratch_shapes=[
            pltpu.VMEM(q_lin.shape, BF16),
            pltpu.VMEM(q_lin.shape, BF16),
            pltpu.VMEM(q_lin.shape, BF16),
            pltpu.VMEM(q_soft.shape, BF16),
            pltpu.VMEM((n, tok, 2 * kvw), BF16),
            pltpu.VMEM((PLANE, heads, DH), F32),
            pltpu.VMEM((per, 2, CHIPS, DH, DH), BF16),
            pltpu.VMEM((per, CHIPS, DH, DH), BF16),
            pltpu.VMEM((per, CHIPS, DH, DH), BF16),
            pltpu.VMEM((per, CHIPS, DH, DH), BF16),
            pltpu.VMEM((per, CHIPS, DH, DH), F32),
            pltpu.VMEM((per, DH, DH), F32),
            pltpu.VMEM((per, DH, DH), BF16),
            pltpu.VMEM((per, DH, DH), BF16),
            pltpu.VMEM((per, CHIPS, DH, DH), BF16),
            pltpu.VMEM((per, CHIPS, DH, DH), BF16),
            pltpu.VMEM((per, CHIPS, DH, DH), BF16),
            pltpu.VMEM((per, 2, CHIPS, DH, DH), BF16),
            pltpu.VMEM((tok, heads * DH), F32),
            pltpu.VMEM((tok, heads), F32),
            pltpu.VMEM((heads, tok), F32),
            pltpu.VMEM((KVH, rows, DH), BF16),
            pltpu.VMEM((KVH, 1, rows), F32),
            pltpu.VMEM((KVH, 1, rows), F32),
            pltpu.VMEM((KVH, DH, rows), F32),
            dma((6,)),
            dma((n,)),
            dma((planes,)),
            dma((planes, CHIPS - 1)),
            dma((planes, CHIPS)),
            dma((PLANE,)),
            dma((PLANE,)),
            dma((per,)),
            dma((per,)),
            dma((per, CHIPS)),
            dma((per, CHIPS)),
            dma((per,)),
            dma((per,)),
            dma((per, CHIPS)),
            dma((per, CHIPS)),
            dma((per,)),
            dma((per,)),
        ],
        compiler_params=pltpu.CompilerParams(
            collective_id=0, has_side_effects=True, vmem_limit_bytes=60 * 1024 * 1024
        ),
        name="both_layers",
    )(q_lin, k_lin, v_lin, log_decay.T, pattern, q_soft, k_soft, v_soft)


def solution(mesh):
    spec = P(("parts", "ctx"), None)
    return jax.shard_map(
        functools.partial(per_device, mesh.shape["ctx"]),
        mesh=mesh,
        in_specs=(spec,) * 8,
        out_specs=(spec, spec),
        check_vma=False,
    )
```
